32 devices in a mesh: mol: 2 (over y), pair: 4 (over z), virt: 2 (over x), rep: 2 (over core).
Axes of the slice: x: 2, y: 2, z: 4, core: 2. Of those that a mesh axis runs over, the one named last changes fastest.
Arguments:
- amplitudes: bfloat16 [12, 32, 384, 384], P(('mol', 'rep'), None, 'pair', 'virt'), parts along dimension 0, may hold values from -6 to 6
- integrals: bfloat16 [64, 384, 32, 384], P('mol', 'virt', 'pair'), parts along dimension 0, may hold values from -0.15625 to 0.15625
- occ_irrep: int32 [32], replicated, may hold values from 0 to 7, as said below
- virt_irrep: int32 [384], replicated, may hold values from 0 to 7, as said below
Outputs:
- cycle_term: float32 [384, 12, 32, 384], P('virt', ('mol', 'rep'), 'pair'), parts along dimension 1
The draws below stay inside these ranges and needn't reach their ends.
There are 2 independent parts, one for each index of `mol`. The reference program is written for one: setup_inputs(seed, part) draws one part's arguments, and reference() takes and returns one part's arrays. A program takes and returns all parts, laid end to end along the dimension named above; an argument that names none is the same for every part. Nothing has to cross between parts.
Inputs may be any that keep to these rules, and one draw needn't show every extreme that they name: `occ_irrep`: labels never fall along the orbitals, the first is 0 and the last is 7. `virt_irrep`: labels never fall along the orbitals, the first is 0 and the last is 7.
All inputs are finite; a program needn't handle non-finite values.
Results may differ from the reference program's by a relative error of at most 0.0003.
Values may be sent and summed in bfloat16 or wider, within the bound.
A program may use at most 192 MiB of HBM per device.

```python
import jax
import jax.numpy as jnp

O = 32
V = 384
OI = 6


def draw_occ_irrep(key, part):
    key = jax.random.fold_in(key, 11)
    labels = jnp.sort(jax.random.randint(key, (O,), 0, 8))
    return labels.at[0].set(0).at[O - 1].set(7).astype(jnp.int32)


def draw_virt_irrep(key, part):
    key = jax.random.fold_in(key, 23)
    labels = jnp.sort(jax.random.randint(key, (V,), 0, 8))
    return labels.at[0].set(0).at[V - 1].set(7).astype(jnp.int32)


def block_levels(own_key, extent, split, smallest, largest):
    def one(dim, parts):
        steps = jax.random.uniform(jax.random.fold_in(jax.random.fold_in(own_key, 6), dim), (parts,), jnp.float32, smallest / len(split), largest / len(split))
        return jnp.repeat(jnp.exp(steps), extent[dim] // parts).reshape((-1,) + (1,) * (len(extent) - dim - 1))

    factor_of = one(*split[0])
    for cut in split[1:]:
        factor_of = factor_of * one(*cut)
    return factor_of


def gaussian(key, dims, scale, most, shards=(), dtype=jnp.bfloat16):
    values = jax.random.normal(key, dims, jnp.float32) * scale
    if len(shards) > 0:
        values = block_levels(key, dims, shards, -0.22, 0.18) * values
    return jnp.clip(values, min=-most, max=most).astype(dtype)


def setup_inputs(seed: int = 0, part: int = 0) -> dict:
    key_list = jax.random.split(jax.random.key(seed), 5)
    part_splits = jax.random.split(jax.random.fold_in(key_list[4], part), 5)
    return {
        "amplitudes": gaussian(part_splits[0], (OI, O, V, V), 1.0, 6.0, ((0, 2), (2, 4), (3, 2))),
        "integrals": gaussian(part_splits[1], (O, V, O, V), (O * V // 8) ** -0.5, 0.15625, ((1, 2), (2, 4))),
        "occ_irrep": draw_occ_irrep(jax.random.fold_in(key_list[4], 71), part),
        "virt_irrep": draw_virt_irrep(jax.random.fold_in(key_list[4], 71), part),
    }


def reference(amplitudes, integrals, occ_irrep, virt_irrep):
    occ_window = occ_irrep[:OI]
    sym_amps = (occ_window[:, None, None, None] ^ occ_irrep[None, :, None, None]
                ^ virt_irrep[None, None, :, None] ^ virt_irrep[None, None, None, :])
    masked_amps = jnp.where(sym_amps == 0, amplitudes, jnp.zeros_like(amplitudes))
    sym_ints = (occ_irrep[:, None, None, None] ^ virt_irrep[None, :, None, None]
                ^ occ_irrep[None, None, :, None] ^ virt_irrep[None, None, None, :])
    masked_ints = jnp.where(sym_ints == 0, integrals, jnp.zeros_like(integrals))
    left = jnp.transpose(masked_amps, (2, 0, 1, 3)).reshape(V * OI, O * V)
    right = masked_ints.reshape(O * V, O * V)
    result = jnp.dot(left, right, preferred_element_type=jnp.float32)
    return result.reshape(V, OI, O, V)
```

```python
import functools

import jax
import jax.numpy as jnp
from jax import lax
from jax.experimental import pallas as pl
from jax.experimental.pallas import tpu as pltpu
from jax.sharding import PartitionSpec as P

LANES = 128
VMEM_LIMIT = 56 * 1024 * 1024


def dense(amplitudes, integrals, sym_i, sym_a, sym_c, sym_j, occ_irrep, virt_irrep):
    sym_amps = (
        sym_i[:, None, None, None]
        ^ occ_irrep[None, :, None, None]
        ^ sym_a[None, None, :, None]
        ^ sym_c[None, None, None, :]
    )
    masked_amps = jnp.where(sym_amps == 0, amplitudes, jnp.zeros_like(amplitudes))
    partial_value = jnp.einsum(
        "ikac,kcjb->aijb",
        lax.all_gather(masked_amps, "pair", axis=2, tiled=True),
        integrals,
        preferred_element_type=jnp.float32,
    )
    cycle_local = lax.psum_scatter(partial_value, "virt", scatter_dimension=0, tiled=True)
    virt_rows = lax.dynamic_slice_in_dim(
        virt_irrep, lax.axis_index("virt") * cycle_local.shape[0], cycle_local.shape[0]
    )
    full_mask = (
        virt_rows[:, None, None, None]
        ^ sym_i[None, :, None, None]
        ^ sym_j[None, None, :, None]
        ^ virt_irrep[None, None, None, :]
    )
    return jnp.where(full_mask == 0, cycle_local, jnp.zeros_like(cycle_local))


def fold_amps_kernel(pack, syms_ref, row_ref, amps_ref, fold_ref, out_ref):
    kks = out_ref.shape[1]
    i = pl.program_id(0)
    labels = row_ref[...]

    @pl.loop(0, kks)
    def _(kk):
        total = None
        for h in range(pack):
            k = kk + h * kks
            keep = labels == syms_ref[i, k]
            block = jnp.where(keep, amps_ref[0, k].astype(jnp.float32), 0.0).astype(jnp.bfloat16)
            term = jnp.dot(block, fold_ref[h], preferred_element_type=jnp.float32)
            total = term if total is None else total + term
        out_ref[0, kk] = total.astype(jnp.bfloat16)


def fold_ints_kernel(pack, occ_ref, table_ref, ints_ref, fold_ref, out_ref, held):
    virts, occs, orbitals = ints_ref.shape[1:]
    label = occ_ref[pl.program_id(0)]
    chunk = 32
    for start in range(0, virts, chunk):
        rows = pl.ds(start, chunk)
        keep = table_ref[rows] == label
        block = jnp.where(keep, ints_ref[0, rows].astype(jnp.float32), 0.0)
        block = block.reshape(chunk * occs, orbitals).astype(jnp.bfloat16)
        held[pl.ds(start * occs, chunk * occs), :] = jnp.dot(
            block, fold_ref[...], preferred_element_type=jnp.float32
        )
    lane = lax.broadcasted_iota(jnp.int32, (virts, LANES), 1)
    for group in range(occs // pack):
        value = held[pl.ds(group * pack, virts, stride=occs), :]
        for h in range(1, pack):
            other = held[pl.ds(group * pack + h, virts, stride=occs), :]
            value = jnp.where(lane < h * (LANES // pack), value, other)
        out_ref[0, 0, :, pl.ds(group * LANES, LANES)] = value.astype(jnp.bfloat16)


def contract_kernel(row_ref, col_ref, amps_ref, unfold_ref, ints_ref, out_ref, block):
    pairs, _, kks, virts, _ = amps_ref.shape
    width = unfold_ref.shape[1]
    for kk in range(kks):
        for p in range(pairs):
            value = jnp.dot(amps_ref[p, 0, kk], unfold_ref[...], preferred_element_type=jnp.float32)
            keep = row_ref[0, pl.ds(p * virts, virts), :] == col_ref[kk]
            block[pl.ds(p * virts, virts), pl.ds(kk * width, width)] = jnp.where(
                keep, value, 0.0
            ).astype(jnp.bfloat16)
    total = jnp.dot(block[...], ints_ref[...], preferred_element_type=jnp.float32)

    @pl.when(pl.program_id(1) == 0)
    def _():
        out_ref[0] = total

    @pl.when(pl.program_id(1) > 0)
    def _():
        out_ref[0] += total


def unfold_kernel(pack, row_ref, col_ref, part_ref, unfold_ref, out_ref):
    occs = out_ref.shape[2]
    for group in range(occs // pack):
        value = part_ref[0, :, pl.ds(group * LANES, LANES)]
        high = value.astype(jnp.bfloat16)
        low = (value - high.astype(jnp.float32)).astype(jnp.bfloat16)
        both = jnp.concatenate([high, low], axis=1)
        for h in range(pack):
            j = group * pack + h
            full = jnp.dot(both, unfold_ref[h], preferred_element_type=jnp.float32)
            out_ref[:, 0, j, :] = jnp.where(row_ref[0] == col_ref[j], full, 0.0)


def params():
    return pltpu.CompilerParams(vmem_limit_bytes=VMEM_LIMIT)


def one_hot(slots, cap, count, dtype=jnp.bfloat16):
    lanes = lax.broadcasted_iota(jnp.int32, (count, 1, LANES), 2)
    shift = lax.broadcasted_iota(jnp.int32, (count, 1, 1), 0) * cap
    return (slots[None, :, None] + shift == lanes).astype(dtype)


def folded(cap, amplitudes, integrals, sym_i, sym_a, sym_c, sym_j, occ_irrep, virt_irrep):
    pack = LANES // cap
    occ_i, occs, virt_a, virt_c = amplitudes.shape
    occ_j, orbitals = integrals.shape[2:]
    kks = occs // pack
    pairs = orbitals // virt_a
    first = jnp.sum((virt_irrep[None, :] < virt_irrep[:, None]).astype(jnp.int32), axis=1)
    slot_b = jnp.arange(orbitals, dtype=jnp.int32) - first
    begin_c = lax.axis_index("virt") * virt_c
    first_c = lax.dynamic_slice_in_dim(first, begin_c, virt_c)
    slot_c = jnp.arange(virt_c, dtype=jnp.int32) + begin_c - jnp.maximum(first_c, begin_c)

    whole = lambda *dims: pl.BlockSpec(dims, lambda *_: (0,) * len(dims))
    smem = pl.BlockSpec(memory_space=pltpu.SMEM)
    fold_c = one_hot(slot_c, cap, pack)
    small = pl.pallas_call(
        functools.partial(fold_amps_kernel, pack),
        grid=(occ_i,),
        in_specs=[
            smem,
            whole(virt_a, virt_c),
            pl.BlockSpec((1, occs, virt_a, virt_c), lambda i: (i, 0, 0, 0)),
            whole(pack, virt_c, LANES),
        ],
        out_specs=pl.BlockSpec((1, kks, virt_a, LANES), lambda i: (i, 0, 0, 0)),
        out_shape=jax.ShapeDtypeStruct((occ_i, kks, virt_a, LANES), jnp.bfloat16),
        compiler_params=params(),
        name="fold_amps",
    )(sym_i[:, None] ^ occ_irrep[None, :], sym_a[:, None] ^ sym_c[None, :], amplitudes, fold_c)
    gathered = lax.all_gather(small, "pair", axis=0)

    fold_b = one_hot(slot_b, cap, pack).sum(0).astype(jnp.bfloat16)
    ints = pl.pallas_call(
        functools.partial(fold_ints_kernel, pack),
        grid=(occs,),
        in_specs=[
            smem,
            whole(virt_c, occ_j, orbitals),
            pl.BlockSpec((1, virt_c, occ_j, orbitals), lambda k: (k, 0, 0, 0)),
            whole(orbitals, LANES),
        ],
        out_specs=pl.BlockSpec((1, 1, virt_c, occ_j * cap), lambda k: (k % kks, k // kks, 0, 0)),
        out_shape=jax.ShapeDtypeStruct((kks, pack, virt_c, occ_j * cap), jnp.bfloat16),
        scratch_shapes=[pltpu.VMEM((virt_c * occ_j, LANES), jnp.float32)],
        compiler_params=params(),
        cost_estimate=pl.CostEstimate(
            flops=2 * integrals.size * 256, bytes_accessed=2 * integrals.size, transcendentals=0
        ),
        name="fold_ints",
    )(
        occ_irrep,
        sym_c[:, None, None] ^ sym_j[None, :, None] ^ virt_irrep[None, None, :],
        integrals,
        fold_b,
    )
    width = pack * virt_c
    ints = ints.reshape(kks * width, occ_j * cap)

    unfold_c = jnp.concatenate([fold_c[h].T for h in range(pack)], axis=1)
    cols = (occ_irrep.reshape(pack, kks).T[:, :, None] ^ sym_c[None, None, :]).reshape(kks, 1, width)
    rows = (sym_i[:, None] ^ virt_irrep[None, :])[:, :, None]
    step = 4 * pack // 2
    step = min(max(step, 2), kks)
    part = pl.pallas_call(
        contract_kernel,
        grid=(occ_i, kks // step),
        in_specs=[
            pl.BlockSpec((1, orbitals, 1), lambda i, s: (i, 0, 0)),
            pl.BlockSpec((step, 1, width), lambda i, s: (s, 0, 0)),
            pl.BlockSpec((pairs, 1, step, virt_a, LANES), lambda i, s: (0, i, s, 0, 0)),
            whole(LANES, width),
            pl.BlockSpec((step * width, occ_j * cap), lambda i, s: (s, 0)),
        ],
        out_specs=pl.BlockSpec((1, orbitals, occ_j * cap), lambda i, s: (i, 0, 0)),
        out_shape=jax.ShapeDtypeStruct((occ_i, orbitals, occ_j * cap), jnp.float32),
        scratch_shapes=[pltpu.VMEM((orbitals, step * width), jnp.bfloat16)],
        compiler_params=params(),
        name="contract",
    )(rows, cols, gathered, unfold_c, ints)

    total = lax.psum_scatter(part, "virt", scatter_dimension=1, tiled=True)
    virt_v = total.shape[1]
    rows_v = lax.dynamic_slice_in_dim(rows, lax.axis_index("virt") * virt_v, virt_v, axis=1)
    cols_b = (sym_j[:, None] ^ virt_irrep[None, :])[:, None, :]
    unfold_b = one_hot(slot_b, cap, pack).transpose(0, 2, 1)
    unfold_b = jnp.concatenate([unfold_b, unfold_b], axis=1)
    return pl.pallas_call(
        functools.partial(unfold_kernel, pack),
        grid=(occ_i,),
        in_specs=[
            pl.BlockSpec((1, virt_v, 1), lambda i: (i, 0, 0)),
            whole(occ_j, 1, orbitals),
            pl.BlockSpec((1, virt_v, occ_j * cap), lambda i: (i, 0, 0)),
            whole(pack, 2 * LANES, orbitals),
        ],
        out_specs=pl.BlockSpec((virt_v, 1, occ_j, orbitals), lambda i: (0, i, 0, 0)),
        out_shape=jax.ShapeDtypeStruct((virt_v, occ_i, occ_j, orbitals), jnp.float32),
        compiler_params=params(),
        name="unfold",
    )(rows_v, cols_b, total, unfold_b)


def shards(amplitudes, integrals, occ_irrep, virt_irrep):
    occ_local, occs, virt_pair, virt_slice = amplitudes.shape
    occ_pair = integrals.shape[2]
    sym_i = lax.dynamic_slice_in_dim(occ_irrep, lax.axis_index("rep") * occ_local, occ_local)
    sym_a = lax.dynamic_slice_in_dim(virt_irrep, lax.axis_index("pair") * virt_pair, virt_pair)
    sym_c = lax.dynamic_slice_in_dim(virt_irrep, lax.axis_index("virt") * virt_slice, virt_slice)
    sym_j = lax.dynamic_slice_in_dim(occ_irrep, lax.axis_index("pair") * occ_pair, occ_pair)
    args = (amplitudes, integrals, sym_i, sym_a, sym_c, sym_j, occ_irrep, virt_irrep)
    fits = (
        occ_pair % 8 == 0
        and virt_pair % 32 == 0
        and virt_slice % 64 == 0
        and occs % 4 == 0
        and virt_irrep.shape[0] % LANES == 0
    )
    if not fits:
        return dense(*args)
    labels = jnp.arange(8, dtype=jnp.int32)
    largest = jnp.max(jnp.sum((virt_irrep[None, :] == labels[:, None]).astype(jnp.int32), axis=1))
    branch = (largest > 64).astype(jnp.int32) + (largest > 128).astype(jnp.int32)
    return lax.switch(
        branch, [functools.partial(folded, 64), functools.partial(folded, 128), dense], *args
    )


def solution(mesh):
    return jax.shard_map(
        shards,
        mesh=mesh,
        in_specs=(
            P(("mol", "rep"), None, "pair", "virt"),
            P("mol", "virt", "pair", None),
            P(),
            P(),
        ),
        out_specs=P("virt", ("mol", "rep"), "pair", None),
        check_vma=False,
    )
```

```python
import functools

import jax
import jax.numpy as jnp
from jax import lax
from jax.experimental import pallas as pl
from jax.experimental.pallas import tpu as pltpu
from jax.sharding import PartitionSpec as P

LANES = 128
VMEM_LIMIT = 56 * 1024 * 1024
SLABS = 3
MESH = pl.DeviceIdType.MESH


def dense(amplitudes, integrals, sym_i, sym_a, sym_c, sym_j, occ_irrep, virt_irrep):
    sym_amps = (
        sym_i[:, None, None, None]
        ^ occ_irrep[None, :, None, None]
        ^ sym_a[None, None, :, None]
        ^ sym_c[None, None, None, :]
    )
    masked_amps = jnp.where(sym_amps == 0, amplitudes, jnp.zeros_like(amplitudes))
    partial_value = jnp.einsum(
        "ikac,kcjb->aijb",
        lax.all_gather(masked_amps, "pair", axis=2, tiled=True),
        integrals,
        preferred_element_type=jnp.float32,
    )
    cycle_local = lax.psum_scatter(partial_value, "virt", scatter_dimension=0, tiled=True)
    virt_rows = lax.dynamic_slice_in_dim(
        virt_irrep, lax.axis_index("virt") * cycle_local.shape[0], cycle_local.shape[0]
    )
    full_mask = (
        virt_rows[:, None, None, None]
        ^ sym_i[None, :, None, None]
        ^ sym_j[None, None, :, None]
        ^ virt_irrep[None, None, None, :]
    )
    return jnp.where(full_mask == 0, cycle_local, jnp.zeros_like(cycle_local))


def cycle_kernel(
    pack,
    occ_ref,
    syms_ref,
    amps_row_ref,
    table_ref,
    row_ref,
    col_ref,
    fold_c_ref,
    fold_b_ref,
    unfold_c_ref,
    amps_ref,
    ints_ref,
    out_ref,
    small,
    ints,
    part,
    arrived,
    block,
    held,
    slab,
    slab_sem,
    send_sem,
    recv_sem,
    part_send_sem,
    part_recv_sem,
):
    pairs, occ_i, kks, virt_a, _ = small.shape
    occs, virts, occ_j, orbitals = ints_ref.shape
    width = unfold_c_ref.shape[1]
    per = pairs // 2
    slots = slab.shape[0]
    me = lax.axis_index("pair")
    side = lax.axis_index("virt")

    barrier = pltpu.get_barrier_semaphore()
    for d in range(1, pairs):
        pl.semaphore_signal(
            barrier, inc=1, device_id={"pair": lax.rem(me + d, pairs)}, device_id_type=MESH
        )
    pl.semaphore_signal(barrier, inc=1, device_id={"virt": 1 - side}, device_id_type=MESH)

    def fetch(k):
        at = lax.rem(k, slots)
        return pltpu.make_async_copy(ints_ref.at[k], slab.at[at], slab_sem.at[at])

    for k in range(slots - 1):
        fetch(k).start()
    pl.semaphore_wait(barrier, pairs)

    def push(i, d):
        return pltpu.make_async_remote_copy(
            src_ref=small.at[me, i],
            dst_ref=small.at[me, i],
            send_sem=send_sem.at[i, d - 1],
            recv_sem=recv_sem.at[i, me],
            device_id={"pair": lax.rem(me + d, pairs)},
            device_id_type=MESH,
        )

    def pull(i, p):
        return pltpu.make_async_remote_copy(
            src_ref=small.at[p, i],
            dst_ref=small.at[p, i],
            send_sem=send_sem.at[i, 0],
            recv_sem=recv_sem.at[i, p],
            device_id={"pair": p},
            device_id_type=MESH,
        )

    @pl.loop(0, occ_i)
    def _(i):
        @pl.loop(0, kks)
        def _(kk):
            total = None
            for h in range(pack):
                k = kk + h * kks
                keep = amps_row_ref[...] == syms_ref[i, k]
                value = jnp.where(keep, amps_ref[i, k].astype(jnp.float32), 0.0)
                term = jnp.dot(
                    value.astype(jnp.bfloat16), fold_c_ref[h], preferred_element_type=jnp.float32
                )
                total = term if total is None else total + term
            small[me, i, kk] = total.astype(jnp.bfloat16)

        for d in range(1, pairs):
            push(i, d).start()

    lane = lax.broadcasted_iota(jnp.int32, (virts, LANES), 1)
    chunk = 32

    @pl.loop(0, occs)
    def _(k):
        @pl.when(k + slots - 1 < occs)
        def _():
            fetch(k + slots - 1).start()

        fetch(k).wait()
        at = lax.rem(k, slots)
        label = occ_ref[k]
        for start in range(0, virts, chunk):
            rows = pl.ds(start, chunk)
            keep = table_ref[rows] == label
            value = jnp.where(keep, slab[at, rows].astype(jnp.float32), 0.0)
            value = value.reshape(chunk * occ_j, orbitals).astype(jnp.bfloat16)
            held[pl.ds(start * occ_j, chunk * occ_j), :] = jnp.dot(
                value, fold_b_ref[...], preferred_element_type=jnp.float32
            )
        base = pl.multiple_of(lax.rem(k, kks) * width + (k // kks) * virts, 16)
        for group in range(occ_j // pack):
            value = held[pl.ds(group * pack, virts, stride=occ_j), :]
            for h in range(1, pack):
                other = held[pl.ds(group * pack + h, virts, stride=occ_j), :]
                value = jnp.where(lane < h * (LANES // pack), value, other)
            ints[pl.ds(base, virts), pl.ds(group * LANES, LANES)] = value.astype(jnp.bfloat16)

    def pass_on(i, q):
        return pltpu.make_async_remote_copy(
            src_ref=part.at[i, (1 - side) * per + q],
            dst_ref=arrived.at[i, q],
            send_sem=part_send_sem.at[i, q],
            recv_sem=part_recv_sem.at[i, q],
            device_id={"virt": 1 - side},
            device_id_type=MESH,
        )

    @pl.loop(0, occ_i * pairs)
    def _(t):
        i = t // pairs
        s = lax.rem(t, pairs)
        q = lax.rem(s, per)
        p = lax.rem(side + 1 + s // per, 2) * per + q

        @pl.when(p != me)
        def _():
            pull(i, p).wait_recv()

        for kk in range(kks):
            value = jnp.dot(
                small[p, i, kk], unfold_c_ref[...], preferred_element_type=jnp.float32
            )
            keep = row_ref[i, p] == col_ref[kk]
            block[:, pl.ds(kk * width, width)] = jnp.where(keep, value, 0.0).astype(jnp.bfloat16)
        part[i, p] = jnp.dot(block[...], ints[...], preferred_element_type=jnp.float32)

        @pl.when(s < per)
        def _():
            pass_on(i, q).start()

    for i in range(occ_i):
        for q in range(per):
            pass_on(i, q).wait()
            out_ref[i, pl.ds(q * virt_a, virt_a), :] = part[i, side * per + q] + arrived[i, q]
    for i in range(occ_i):
        for d in range(1, pairs):
            push(i, d).wait_send()


def unfold_kernel(pack, row_ref, col_ref, part_ref, unfold_ref, out_ref):
    occs = out_ref.shape[2]
    for group in range(occs // pack):
        value = part_ref[0, :, pl.ds(group * LANES, LANES)]
        high = value.astype(jnp.bfloat16)
        low = (value - high.astype(jnp.float32)).astype(jnp.bfloat16)
        both = jnp.concatenate([high, low], axis=1)
        for h in range(pack):
            j = group * pack + h
            full = jnp.dot(both, unfold_ref[h], preferred_element_type=jnp.float32)
            out_ref[:, 0, j, :] = jnp.where(row_ref[0] == col_ref[j], full, 0.0)


def params():
    return pltpu.CompilerParams(vmem_limit_bytes=VMEM_LIMIT)


def one_hot(slots, cap, count, dtype=jnp.bfloat16):
    lanes = lax.broadcasted_iota(jnp.int32, (count, 1, LANES), 2)
    shift = lax.broadcasted_iota(jnp.int32, (count, 1, 1), 0) * cap
    return (slots[None, :, None] + shift == lanes).astype(dtype)


def folded(cap, amplitudes, integrals, sym_i, sym_a, sym_c, sym_j, occ_irrep, virt_irrep):
    pack = LANES // cap
    occ_i, occs, virt_a, virt_c = amplitudes.shape
    occ_j, orbitals = integrals.shape[2:]
    kks = occs // pack
    pairs = orbitals // virt_a
    first = jnp.sum((virt_irrep[None, :] < virt_irrep[:, None]).astype(jnp.int32), axis=1)
    slot_b = jnp.arange(orbitals, dtype=jnp.int32) - first
    begin_c = lax.axis_index("virt") * virt_c
    first_c = lax.dynamic_slice_in_dim(first, begin_c, virt_c)
    slot_c = jnp.arange(virt_c, dtype=jnp.int32) + begin_c - jnp.maximum(first_c, begin_c)

    whole = lambda *dims: pl.BlockSpec(dims, lambda *_: (0,) * len(dims))
    smem = pl.BlockSpec(memory_space=pltpu.SMEM)
    fold_c = one_hot(slot_c, cap, pack)
    fold_b = one_hot(slot_b, cap, pack).sum(0).astype(jnp.bfloat16)
    width = pack * virt_c
    unfold_c = jnp.concatenate([fold_c[h].T for h in range(pack)], axis=1)
    cols = (occ_irrep.reshape(pack, kks).T[:, :, None] ^ sym_c[None, None, :]).reshape(kks, 1, width)
    rows = (sym_i[:, None] ^ virt_irrep[None, :])[:, :, None]
    vmem = pl.BlockSpec(memory_space=pltpu.VMEM)
    wide = occ_j * cap
    total = pl.pallas_call(
        functools.partial(cycle_kernel, pack),
        in_specs=[smem, smem] + [vmem] * 8 + [pl.BlockSpec(memory_space=pl.ANY)],
        out_specs=vmem,
        out_shape=jax.ShapeDtypeStruct((occ_i, orbitals // 2, wide), jnp.float32),
        scratch_shapes=[
            pltpu.VMEM((pairs, occ_i, kks, virt_a, LANES), jnp.bfloat16),
            pltpu.VMEM((kks * width, wide), jnp.bfloat16),
            pltpu.VMEM((occ_i, pairs, virt_a, wide), jnp.float32),
            pltpu.VMEM((occ_i, pairs // 2, virt_a, wide), jnp.float32),
            pltpu.VMEM((virt_a, kks * width), jnp.bfloat16),
            pltpu.VMEM((virt_c * occ_j, LANES), jnp.float32),
            pltpu.VMEM((SLABS, virt_c, occ_j, orbitals), jnp.bfloat16),
            pltpu.SemaphoreType.DMA((SLABS,)),
            pltpu.SemaphoreType.DMA((occ_i, pairs - 1)),
            pltpu.SemaphoreType.DMA((occ_i, pairs)),
            pltpu.SemaphoreType.DMA((occ_i, pairs // 2)),
            pltpu.SemaphoreType.DMA((occ_i, pairs // 2)),
        ],
        compiler_params=pltpu.CompilerParams(
            vmem_limit_bytes=VMEM_LIMIT, collective_id=pack, has_side_effects=True
        ),
        cost_estimate=pl.CostEstimate(
            flops=2 * integrals.size * 256, bytes_accessed=2 * integrals.size, transcendentals=0
        ),
        name="cycle",
    )(
        occ_irrep,
        sym_i[:, None] ^ occ_irrep[None, :],
        sym_a[:, None] ^ sym_c[None, :],
        sym_c[:, None, None] ^ sym_j[None, :, None] ^ virt_irrep[None, None, :],
        rows.reshape(occ_i, pairs, virt_a, 1),
        cols,
        fold_c,
        fold_b,
        unfold_c,
        amplitudes,
        integrals,
    )

    virt_v = total.shape[1]
    rows_v = lax.dynamic_slice_in_dim(rows, lax.axis_index("virt") * virt_v, virt_v, axis=1)
    cols_b = (sym_j[:, None] ^ virt_irrep[None, :])[:, None, :]
    unfold_b = one_hot(slot_b, cap, pack).transpose(0, 2, 1)
    unfold_b = jnp.concatenate([unfold_b, unfold_b], axis=1)
    return pl.pallas_call(
        functools.partial(unfold_kernel, pack),
        grid=(occ_i,),
        in_specs=[
            pl.BlockSpec((1, virt_v, 1), lambda i: (i, 0, 0)),
            whole(occ_j, 1, orbitals),
            pl.BlockSpec((1, virt_v, occ_j * cap), lambda i: (i, 0, 0)),
            whole(pack, 2 * LANES, orbitals),
        ],
        out_specs=pl.BlockSpec((virt_v, 1, occ_j, orbitals), lambda i: (0, i, 0, 0)),
        out_shape=jax.ShapeDtypeStruct((virt_v, occ_i, occ_j, orbitals), jnp.float32),
        compiler_params=params(),
        name="unfold",
    )(rows_v, cols_b, total, unfold_b)


def shards(mesh, amplitudes, integrals, occ_irrep, virt_irrep):
    occ_local, occs, virt_pair, virt_slice = amplitudes.shape
    occ_pair = integrals.shape[2]
    sym_i = lax.dynamic_slice_in_dim(occ_irrep, lax.axis_index("rep") * occ_local, occ_local)
    sym_a = lax.dynamic_slice_in_dim(virt_irrep, lax.axis_index("pair") * virt_pair, virt_pair)
    sym_c = lax.dynamic_slice_in_dim(virt_irrep, lax.axis_index("virt") * virt_slice, virt_slice)
    sym_j = lax.dynamic_slice_in_dim(occ_irrep, lax.axis_index("pair") * occ_pair, occ_pair)
    args = (amplitudes, integrals, sym_i, sym_a, sym_c, sym_j, occ_irrep, virt_irrep)
    fits = (
        mesh.shape["virt"] == 2
        and mesh.shape["pair"] % 2 == 0
        and occ_pair % 8 == 0
        and virt_pair % 32 == 0
        and virt_slice % 64 == 0
        and occs % 4 == 0
        and virt_irrep.shape[0] % LANES == 0
    )
    if not fits:
        return dense(*args)
    labels = jnp.arange(8, dtype=jnp.int32)
    largest = jnp.max(jnp.sum((virt_irrep[None, :] == labels[:, None]).astype(jnp.int32), axis=1))
    branch = (largest > 64).astype(jnp.int32) + (largest > 128).astype(jnp.int32)
    return lax.switch(
        branch, [functools.partial(folded, 64), functools.partial(folded, 128), dense], *args
    )


def solution(mesh):
    return jax.shard_map(
        functools.partial(shards, mesh),
        mesh=mesh,
        in_specs=(
            P(("mol", "rep"), None, "pair", "virt"),
            P("mol", "virt", "pair", None),
            P(),
            P(),
        ),
        out_specs=P("virt", ("mol", "rep"), "pair", None),
        check_vma=False,
    )
```

```python
import functools

import jax
import jax.numpy as jnp
from jax import lax
from jax.experimental import pallas as pl
from jax.experimental.pallas import tpu as pltpu
from jax.sharding import PartitionSpec as P

LANES = 128
VMEM_LIMIT = 56 * 1024 * 1024
SLABS = 3
MESH = pl.DeviceIdType.MESH


def dense(amplitudes, integrals, sym_i, sym_a, sym_c, sym_j, occ_irrep, virt_irrep):
    sym_amps = (
        sym_i[:, None, None, None]
        ^ occ_irrep[None, :, None, None]
        ^ sym_a[None, None, :, None]
        ^ sym_c[None, None, None, :]
    )
    masked_amps = jnp.where(sym_amps == 0, amplitudes, jnp.zeros_like(amplitudes))
    partial_value = jnp.einsum(
        "ikac,kcjb->aijb",
        lax.all_gather(masked_amps, "pair", axis=2, tiled=True),
        integrals,
        preferred_element_type=jnp.float32,
    )
    cycle_local = lax.psum_scatter(partial_value, "virt", scatter_dimension=0, tiled=True)
    virt_rows = lax.dynamic_slice_in_dim(
        virt_irrep, lax.axis_index("virt") * cycle_local.shape[0], cycle_local.shape[0]
    )
    full_mask = (
        virt_rows[:, None, None, None]
        ^ sym_i[None, :, None, None]
        ^ sym_j[None, None, :, None]
        ^ virt_irrep[None, None, None, :]
    )
    return jnp.where(full_mask == 0, cycle_local, jnp.zeros_like(cycle_local))


def cycle_kernel(
    pack,
    occ_ref,
    syms_ref,
    amps_row_ref,
    table_ref,
    row_ref,
    col_ref,
    fold_c_ref,
    fold_b_ref,
    unfold_c_ref,
    amps_ref,
    ints_ref,
    out_ref,
    small,
    ints,
    part,
    arrived,
    block,
    held,
    slab,
    slab_sem,
    send_sem,
    recv_sem,
    part_send_sem,
    part_recv_sem,
):
    pairs, occ_i, kks, virt_a, _ = small.shape
    occs, virts, occ_j, orbitals = ints_ref.shape
    width = unfold_c_ref.shape[1]
    per = pairs // 2
    slots = slab.shape[0]
    me = lax.axis_index("pair")
    side = lax.axis_index("virt")

    barrier = pltpu.get_barrier_semaphore()
    for d in range(1, pairs):
        pl.semaphore_signal(
            barrier, inc=1, device_id={"pair": lax.rem(me + d, pairs)}, device_id_type=MESH
        )
    pl.semaphore_signal(barrier, inc=1, device_id={"virt": 1 - side}, device_id_type=MESH)

    def fetch(k):
        at = lax.rem(k, slots)
        return pltpu.make_async_copy(ints_ref.at[k], slab.at[at], slab_sem.at[at])

    for k in range(slots - 1):
        fetch(k).start()
    pl.semaphore_wait(barrier, pairs)

    inner = jnp.logical_and(me > 0, me < pairs - 1)

    def hop(i, src, dst, sem):
        return pltpu.make_async_remote_copy(
            src_ref=small.at[src, i],
            dst_ref=small.at[src, i],
            send_sem=send_sem.at[i, sem],
            recv_sem=recv_sem.at[i, src],
            device_id={"pair": dst},
            device_id_type=MESH,
        )

    def forward_near(i):
        @pl.when(inner)
        def _():
            hop(i, me - 1, me + 1, 2).wait_recv()
            hop(i, me - 1, me + 1, 2).start()
            hop(i, me + 1, me - 1, 3).wait_recv()
            hop(i, me + 1, me - 1, 3).start()

    def far_hop(i):
        src = 6 - 3 * me
        return hop(i, src, 3 - src, 4)

    def forward_far(i):
        @pl.when(inner)
        def _():
            far_hop(i).wait_recv()
            far_hop(i).start()

    @pl.loop(0, occ_i)
    def _(i):
        @pl.loop(0, kks)
        def _(kk):
            total = None
            for h in range(pack):
                k = kk + h * kks
                keep = amps_row_ref[...] == syms_ref[i, k]
                value = jnp.where(keep, amps_ref[i, k].astype(jnp.float32), 0.0)
                term = jnp.dot(
                    value.astype(jnp.bfloat16), fold_c_ref[h], preferred_element_type=jnp.float32
                )
                total = term if total is None else total + term
            small[me, i, kk] = total.astype(jnp.bfloat16)

        @pl.when(me < pairs - 1)
        def _():
            hop(i, me, me + 1, 0).start()

        @pl.when(me > 0)
        def _():
            hop(i, me, me - 1, 1).start()

    lane = lax.broadcasted_iota(jnp.int32, (virts, LANES), 1)
    chunk = 32

    @pl.loop(0, occs)
    def _(k):
        @pl.when(k + slots - 1 < occs)
        def _():
            fetch(k + slots - 1).start()

        for i in range(occ_i):
            @pl.when(k == 3 + 8 * i)
            def _():
                forward_near(i)

        fetch(k).wait()
        at = lax.rem(k, slots)
        label = occ_ref[k]
        for start in range(0, virts, chunk):
            rows = pl.ds(start, chunk)
            keep = table_ref[rows] == label
            value = jnp.where(keep, slab[at, rows].astype(jnp.float32), 0.0)
            value = value.reshape(chunk * occ_j, orbitals).astype(jnp.bfloat16)
            held[pl.ds(start * occ_j, chunk * occ_j), :] = jnp.dot(
                value, fold_b_ref[...], preferred_element_type=jnp.float32
            )
        base = pl.multiple_of(lax.rem(k, kks) * width + (k // kks) * virts, 16)
        for group in range(occ_j // pack):
            value = held[pl.ds(group * pack, virts, stride=occ_j), :]
            for h in range(1, pack):
                other = held[pl.ds(group * pack + h, virts, stride=occ_j), :]
                value = jnp.where(lane < h * (LANES // pack), value, other)
            ints[pl.ds(base, virts), pl.ds(group * LANES, LANES)] = value.astype(jnp.bfloat16)

    def pass_on(i, q):
        return pltpu.make_async_remote_copy(
            src_ref=part.at[i, (1 - side) * per + q],
            dst_ref=arrived.at[i, q],
            send_sem=part_send_sem.at[i, q],
            recv_sem=part_recv_sem.at[i, q],
            device_id={"virt": 1 - side},
            device_id_type=MESH,
        )

    @pl.loop(0, occ_i * pairs)
    def _(t):
        far = t // occ_i
        i = lax.rem(t, occ_i)
        low = me < 2
        p = jnp.where(
            far == 0,
            me,
            jnp.where(
                far == 1,
                jnp.where(low, 1 - me, 5 - me),
                jnp.where(far == 2, jnp.where(low, 2, 1), jnp.where(low, 3, 0)),
            ),
        )
        q = lax.rem(p, per)

        @pl.when(far == 1)
        def _():
            forward_far(i)

        @pl.when(jnp.logical_and(p != me, jnp.logical_not(inner)))
        def _():
            hop(i, p, p, 0).wait_recv()

        for kk in range(kks):
            value = jnp.dot(
                small[p, i, kk], unfold_c_ref[...], preferred_element_type=jnp.float32
            )
            keep = row_ref[i, p] == col_ref[kk]
            block[:, pl.ds(kk * width, width)] = jnp.where(keep, value, 0.0).astype(jnp.bfloat16)
        part[i, p] = jnp.dot(block[...], ints[...], preferred_element_type=jnp.float32)

        @pl.when(p // per != side)
        def _():
            pass_on(i, q).start()

    for i in range(occ_i):
        for q in range(per):
            pass_on(i, q).wait()
            out_ref[i, pl.ds(q * virt_a, virt_a), :] = part[i, side * per + q] + arrived[i, q]
    for i in range(occ_i):
        @pl.when(me < pairs - 1)
        def _():
            hop(i, me, me + 1, 0).wait_send()

        @pl.when(me > 0)
        def _():
            hop(i, me, me - 1, 1).wait_send()

        @pl.when(inner)
        def _():
            hop(i, me - 1, me + 1, 2).wait_send()
            hop(i, me + 1, me - 1, 3).wait_send()
            far_hop(i).wait_send()


def unfold_kernel(pack, row_ref, col_ref, part_ref, unfold_ref, out_ref):
    occs = out_ref.shape[2]
    for group in range(occs // pack):
        value = part_ref[0, :, pl.ds(group * LANES, LANES)]
        high = value.astype(jnp.bfloat16)
        low = (value - high.astype(jnp.float32)).astype(jnp.bfloat16)
        both = jnp.concatenate([high, low], axis=1)
        for h in range(pack):
            j = group * pack + h
            full = jnp.dot(both, unfold_ref[h], preferred_element_type=jnp.float32)
            out_ref[:, 0, j, :] = jnp.where(row_ref[0] == col_ref[j], full, 0.0)


def params():
    return pltpu.CompilerParams(vmem_limit_bytes=VMEM_LIMIT)


def one_hot(slots, cap, count, dtype=jnp.bfloat16):
    lanes = lax.broadcasted_iota(jnp.int32, (count, 1, LANES), 2)
    shift = lax.broadcasted_iota(jnp.int32, (count, 1, 1), 0) * cap
    return (slots[None, :, None] + shift == lanes).astype(dtype)


def folded(cap, amplitudes, integrals, sym_i, sym_a, sym_c, sym_j, occ_irrep, virt_irrep):
    pack = LANES // cap
    occ_i, occs, virt_a, virt_c = amplitudes.shape
    occ_j, orbitals = integrals.shape[2:]
    kks = occs // pack
    pairs = orbitals // virt_a
    first = jnp.sum((virt_irrep[None, :] < virt_irrep[:, None]).astype(jnp.int32), axis=1)
    slot_b = jnp.arange(orbitals, dtype=jnp.int32) - first
    begin_c = lax.axis_index("virt") * virt_c
    first_c = lax.dynamic_slice_in_dim(first, begin_c, virt_c)
    slot_c = jnp.arange(virt_c, dtype=jnp.int32) + begin_c - jnp.maximum(first_c, begin_c)

    whole = lambda *dims: pl.BlockSpec(dims, lambda *_: (0,) * len(dims))
    smem = pl.BlockSpec(memory_space=pltpu.SMEM)
    fold_c = one_hot(slot_c, cap, pack)
    fold_b = one_hot(slot_b, cap, pack).sum(0).astype(jnp.bfloat16)
    width = pack * virt_c
    unfold_c = jnp.concatenate([fold_c[h].T for h in range(pack)], axis=1)
    cols = (occ_irrep.reshape(pack, kks).T[:, :, None] ^ sym_c[None, None, :]).reshape(kks, 1, width)
    rows = (sym_i[:, None] ^ virt_irrep[None, :])[:, :, None]
    vmem = pl.BlockSpec(memory_space=pltpu.VMEM)
    wide = occ_j * cap
    total = pl.pallas_call(
        functools.partial(cycle_kernel, pack),
        in_specs=[smem, smem] + [vmem] * 8 + [pl.BlockSpec(memory_space=pl.ANY)],
        out_specs=vmem,
        out_shape=jax.ShapeDtypeStruct((occ_i, orbitals // 2, wide), jnp.float32),
        scratch_shapes=[
            pltpu.VMEM((pairs, occ_i, kks, virt_a, LANES), jnp.bfloat16),
            pltpu.VMEM((kks * width, wide), jnp.bfloat16),
            pltpu.VMEM((occ_i, pairs, virt_a, wide), jnp.float32),
            pltpu.VMEM((occ_i, pairs // 2, virt_a, wide), jnp.float32),
            pltpu.VMEM((virt_a, kks * width), jnp.bfloat16),
            pltpu.VMEM((virt_c * occ_j, LANES), jnp.float32),
            pltpu.VMEM((SLABS, virt_c, occ_j, orbitals), jnp.bfloat16),
            pltpu.SemaphoreType.DMA((SLABS,)),
            pltpu.SemaphoreType.DMA((occ_i, 5)),
            pltpu.SemaphoreType.DMA((occ_i, pairs)),
            pltpu.SemaphoreType.DMA((occ_i, pairs // 2)),
            pltpu.SemaphoreType.DMA((occ_i, pairs // 2)),
        ],
        compiler_params=pltpu.CompilerParams(
            vmem_limit_bytes=VMEM_LIMIT, collective_id=pack, has_side_effects=True
        ),
        cost_estimate=pl.CostEstimate(
            flops=2 * integrals.size * 256, bytes_accessed=2 * integrals.size, transcendentals=0
        ),
        name="cycle",
    )(
        occ_irrep,
        sym_i[:, None] ^ occ_irrep[None, :],
        sym_a[:, None] ^ sym_c[None, :],
        sym_c[:, None, None] ^ sym_j[None, :, None] ^ virt_irrep[None, None, :],
        rows.reshape(occ_i, pairs, virt_a, 1),
        cols,
        fold_c,
        fold_b,
        unfold_c,
        amplitudes,
        integrals,
    )

    virt_v = total.shape[1]
    rows_v = lax.dynamic_slice_in_dim(rows, lax.axis_index("virt") * virt_v, virt_v, axis=1)
    cols_b = (sym_j[:, None] ^ virt_irrep[None, :])[:, None, :]
    unfold_b = one_hot(slot_b, cap, pack).transpose(0, 2, 1)
    unfold_b = jnp.concatenate([unfold_b, unfold_b], axis=1)
    return pl.pallas_call(
        functools.partial(unfold_kernel, pack),
        grid=(occ_i,),
        in_specs=[
            pl.BlockSpec((1, virt_v, 1), lambda i: (i, 0, 0)),
            whole(occ_j, 1, orbitals),
            pl.BlockSpec((1, virt_v, occ_j * cap), lambda i: (i, 0, 0)),
            whole(pack, 2 * LANES, orbitals),
        ],
        out_specs=pl.BlockSpec((virt_v, 1, occ_j, orbitals), lambda i: (0, i, 0, 0)),
        out_shape=jax.ShapeDtypeStruct((virt_v, occ_i, occ_j, orbitals), jnp.float32),
        compiler_params=params(),
        name="unfold",
    )(rows_v, cols_b, total, unfold_b)


def shards(mesh, amplitudes, integrals, occ_irrep, virt_irrep):
    occ_local, occs, virt_pair, virt_slice = amplitudes.shape
    occ_pair = integrals.shape[2]
    sym_i = lax.dynamic_slice_in_dim(occ_irrep, lax.axis_index("rep") * occ_local, occ_local)
    sym_a = lax.dynamic_slice_in_dim(virt_irrep, lax.axis_index("pair") * virt_pair, virt_pair)
    sym_c = lax.dynamic_slice_in_dim(virt_irrep, lax.axis_index("virt") * virt_slice, virt_slice)
    sym_j = lax.dynamic_slice_in_dim(occ_irrep, lax.axis_index("pair") * occ_pair, occ_pair)
    args = (amplitudes, integrals, sym_i, sym_a, sym_c, sym_j, occ_irrep, virt_irrep)
    fits = (
        mesh.shape["virt"] == 2
        and mesh.shape["pair"] == 4
        and occ_pair % 8 == 0
        and virt_pair % 32 == 0
        and virt_slice % 64 == 0
        and occs % 4 == 0
        and virt_irrep.shape[0] % LANES == 0
    )
    if not fits:
        return dense(*args)
    labels = jnp.arange(8, dtype=jnp.int32)
    largest = jnp.max(jnp.sum((virt_irrep[None, :] == labels[:, None]).astype(jnp.int32), axis=1))
    branch = (largest > 64).astype(jnp.int32) + (largest > 128).astype(jnp.int32)
    return lax.switch(
        branch, [functools.partial(folded, 64), functools.partial(folded, 128), dense], *args
    )


def solution(mesh):
    return jax.shard_map(
        functools.partial(shards, mesh),
        mesh=mesh,
        in_specs=(
            P(("mol", "rep"), None, "pair", "virt"),
            P("mol", "virt", "pair", None),
            P(),
            P(),
        ),
        out_specs=P("virt", ("mol", "rep"), "pair", None),
        check_vma=False,
    )
```

```python
import functools

import jax
import jax.numpy as jnp
from jax import lax
from jax.experimental import pallas as pl
from jax.experimental.pallas import tpu as pltpu
from jax.sharding import PartitionSpec as P

LANES = 128
VMEM_LIMIT = 56 * 1024 * 1024
SLABS = 3
MESH = pl.DeviceIdType.MESH


def dense(amplitudes, integrals, sym_i, sym_a, sym_c, sym_j, occ_irrep, virt_irrep):
    sym_amps = (
        sym_i[:, None, None, None]
        ^ occ_irrep[None, :, None, None]
        ^ sym_a[None, None, :, None]
        ^ sym_c[None, None, None, :]
    )
    masked_amps = jnp.where(sym_amps == 0, amplitudes, jnp.zeros_like(amplitudes))
    partial_value = jnp.einsum(
        "ikac,kcjb->aijb",
        lax.all_gather(masked_amps, "pair", axis=2, tiled=True),
        integrals,
        preferred_element_type=jnp.float32,
    )
    cycle_local = lax.psum_scatter(partial_value, "virt", scatter_dimension=0, tiled=True)
    virt_rows = lax.dynamic_slice_in_dim(
        virt_irrep, lax.axis_index("virt") * cycle_local.shape[0], cycle_local.shape[0]
    )
    full_mask = (
        virt_rows[:, None, None, None]
        ^ sym_i[None, :, None, None]
        ^ sym_j[None, None, :, None]
        ^ virt_irrep[None, None, None, :]
    )
    return jnp.where(full_mask == 0, cycle_local, jnp.zeros_like(cycle_local))


def cycle_kernel(
    pack,
    occ_ref,
    syms_ref,
    amps_row_ref,
    table_ref,
    row_ref,
    col_ref,
    fold_c_ref,
    fold_b_ref,
    unfold_c_ref,
    amps_ref,
    ints_ref,
    out_ref,
    small,
    ints,
    part,
    arrived,
    block,
    held,
    slab,
    slab_sem,
    send_sem,
    recv_sem,
    part_send_sem,
    part_recv_sem,
):
    pairs, occ_i, kks, virt_a, _ = small.shape
    occs, virts, occ_j, orbitals = ints_ref.shape
    width = unfold_c_ref.shape[1]
    per = pairs // 2
    slots = slab.shape[0]
    me = lax.axis_index("pair")
    side = lax.axis_index("virt")

    barrier = pltpu.get_barrier_semaphore()
    for d in range(1, pairs):
        pl.semaphore_signal(
            barrier, inc=1, device_id={"pair": lax.rem(me + d, pairs)}, device_id_type=MESH
        )
    pl.semaphore_signal(barrier, inc=1, device_id={"virt": 1 - side}, device_id_type=MESH)

    def fetch(k):
        at = lax.rem(k, slots)
        return pltpu.make_async_copy(ints_ref.at[k], slab.at[at], slab_sem.at[at])

    for k in range(slots - 1):
        fetch(k).start()
    pl.semaphore_wait(barrier, pairs)

    inner = jnp.logical_and(me > 0, me < pairs - 1)

    def hop(i, src, dst, sem):
        return pltpu.make_async_remote_copy(
            src_ref=small.at[src, i],
            dst_ref=small.at[src, i],
            send_sem=send_sem.at[i, sem],
            recv_sem=recv_sem.at[i, src],
            device_id={"pair": dst},
            device_id_type=MESH,
        )

    def forward_near(i):
        @pl.when(inner)
        def _():
            hop(i, me - 1, me + 1, 2).wait_recv()
            hop(i, me - 1, me + 1, 2).start()
            hop(i, me + 1, me - 1, 3).wait_recv()
            hop(i, me + 1, me - 1, 3).start()

    def far_hop(i):
        src = 6 - 3 * me
        return hop(i, src, 3 - src, 4)

    def forward_far(i):
        @pl.when(inner)
        def _():
            far_hop(i).wait_recv()
            far_hop(i).start()

    @pl.loop(0, occ_i)
    def _(i):
        @pl.loop(0, kks)
        def _(kk):
            total = None
            for h in range(pack):
                k = kk + h * kks
                keep = amps_row_ref[...] == (syms_ref[i] ^ occ_ref[k])
                value = jnp.where(keep, amps_ref[i, k].astype(jnp.float32), 0.0)
                term = jnp.dot(
                    value.astype(jnp.bfloat16), fold_c_ref[h], preferred_element_type=jnp.float32
                )
                total = term if total is None else total + term
            small[me, i, kk] = total.astype(jnp.bfloat16)

        @pl.when(me < pairs - 1)
        def _():
            hop(i, me, me + 1, 0).start()

        @pl.when(me > 0)
        def _():
            hop(i, me, me - 1, 1).start()

    lane = lax.broadcasted_iota(jnp.int32, (virts, LANES), 1)
    chunk = 32

    @pl.loop(0, occs)
    def _(k):
        @pl.when(k + slots - 1 < occs)
        def _():
            fetch(k + slots - 1).start()

        for i in range(occ_i):
            @pl.when(k == 3 + 8 * i)
            def _():
                forward_near(i)

        fetch(k).wait()
        at = lax.rem(k, slots)
        label = occ_ref[k]
        for start in range(0, virts, chunk):
            rows = pl.ds(start, chunk)
            keep = table_ref[rows] == label
            value = jnp.where(keep, slab[at, rows].astype(jnp.float32), 0.0)
            value = value.reshape(chunk * occ_j, orbitals).astype(jnp.bfloat16)
            held[pl.ds(start * occ_j, chunk * occ_j), :] = jnp.dot(
                value, fold_b_ref[...], preferred_element_type=jnp.float32
            )
        base = pl.multiple_of(lax.rem(k, kks) * width + (k // kks) * virts, 16)
        for group in range(occ_j // pack):
            value = held[pl.ds(group * pack, virts, stride=occ_j), :]
            for h in range(1, pack):
                other = held[pl.ds(group * pack + h, virts, stride=occ_j), :]
                value = jnp.where(lane < h * (LANES // pack), value, other)
            ints[pl.ds(base, virts), pl.ds(group * LANES, LANES)] = value.astype(jnp.bfloat16)

    def pass_on(i, q):
        return pltpu.make_async_remote_copy(
            src_ref=part.at[i, (1 - side) * per + q],
            dst_ref=arrived.at[i, q],
            send_sem=part_send_sem.at[i, q],
            recv_sem=part_recv_sem.at[i, q],
            device_id={"virt": 1 - side},
            device_id_type=MESH,
        )

    place = lax.broadcasted_iota(jnp.int32, (1, width), 1)

    @pl.loop(0, occ_i * pairs)
    def _(t):
        far = t // occ_i
        i = lax.rem(t, occ_i)
        low = me < 2
        p = jnp.where(
            far == 0,
            me,
            jnp.where(
                far == 1,
                jnp.where(low, 1 - me, 5 - me),
                jnp.where(far == 2, jnp.where(low, 2, 1), jnp.where(low, 3, 0)),
            ),
        )
        q = lax.rem(p, per)

        @pl.when(far == 1)
        def _():
            forward_far(i)

        @pl.when(jnp.logical_and(p != me, jnp.logical_not(inner)))
        def _():
            hop(i, p, p, 0).wait_recv()

        for kk in range(kks):
            value = jnp.dot(
                small[p, i, kk], unfold_c_ref[...], preferred_element_type=jnp.float32
            )
            label = occ_ref[kk]
            for h in range(1, pack):
                label = jnp.where(place < h * virts, label, occ_ref[kk + h * kks])
            keep = row_ref[i, p] == (col_ref[...] ^ label)
            block[:, pl.ds(kk * width, width)] = jnp.where(keep, value, 0.0).astype(jnp.bfloat16)
        part[i, p] = jnp.dot(block[...], ints[...], preferred_element_type=jnp.float32)

        @pl.when(p // per != side)
        def _():
            pass_on(i, q).start()

    for i in range(occ_i):
        for q in range(per):
            pass_on(i, q).wait()
            out_ref[i, pl.ds(q * virt_a, virt_a), :] = part[i, side * per + q] + arrived[i, q]
    for i in range(occ_i):
        @pl.when(me < pairs - 1)
        def _():
            hop(i, me, me + 1, 0).wait_send()

        @pl.when(me > 0)
        def _():
            hop(i, me, me - 1, 1).wait_send()

        @pl.when(inner)
        def _():
            hop(i, me - 1, me + 1, 2).wait_send()
            hop(i, me + 1, me - 1, 3).wait_send()
            far_hop(i).wait_send()


def unfold_kernel(pack, row_ref, col_ref, part_ref, unfold_ref, out_ref):
    occs = out_ref.shape[2]
    for group in range(occs // pack):
        value = part_ref[0, :, pl.ds(group * LANES, LANES)]
        high = value.astype(jnp.bfloat16)
        low = (value - high.astype(jnp.float32)).astype(jnp.bfloat16)
        both = jnp.concatenate([high, low], axis=1)
        for h in range(pack):
            j = group * pack + h
            full = jnp.dot(both, unfold_ref[h], preferred_element_type=jnp.float32)
            out_ref[:, 0, j, :] = jnp.where(row_ref[0] == col_ref[j], full, 0.0)


def params():
    return pltpu.CompilerParams(vmem_limit_bytes=VMEM_LIMIT)


def one_hot(slots, cap, count, dtype=jnp.bfloat16):
    lanes = lax.broadcasted_iota(jnp.int32, (count, 1, LANES), 2)
    shift = lax.broadcasted_iota(jnp.int32, (count, 1, 1), 0) * cap
    return (slots[None, :, None] + shift == lanes).astype(dtype)


def folded(cap, amplitudes, integrals, sym_i, sym_a, sym_c, sym_j, occ_irrep, virt_irrep):
    pack = LANES // cap
    occ_i, occs, virt_a, virt_c = amplitudes.shape
    occ_j, orbitals = integrals.shape[2:]
    kks = occs // pack
    pairs = orbitals // virt_a
    first = jnp.sum((virt_irrep[None, :] < virt_irrep[:, None]).astype(jnp.int32), axis=1)
    slot_b = jnp.arange(orbitals, dtype=jnp.int32) - first
    begin_c = lax.axis_index("virt") * virt_c
    first_c = lax.dynamic_slice_in_dim(first, begin_c, virt_c)
    slot_c = jnp.arange(virt_c, dtype=jnp.int32) + begin_c - jnp.maximum(first_c, begin_c)

    whole = lambda *dims: pl.BlockSpec(dims, lambda *_: (0,) * len(dims))
    smem = pl.BlockSpec(memory_space=pltpu.SMEM)
    fold_c = one_hot(slot_c, cap, pack)
    fold_b = one_hot(slot_b, cap, pack).sum(0).astype(jnp.bfloat16)
    width = pack * virt_c
    unfold_c = jnp.concatenate([fold_c[h].T for h in range(pack)], axis=1)
    cols = jnp.concatenate([sym_c] * pack)[None, :]
    rows = (sym_i[:, None] ^ virt_irrep[None, :])[:, :, None]
    vmem = pl.BlockSpec(memory_space=pltpu.VMEM)
    wide = occ_j * cap
    total = pl.pallas_call(
        functools.partial(cycle_kernel, pack),
        in_specs=[smem, smem] + [vmem] * 8 + [pl.BlockSpec(memory_space=pl.ANY)],
        out_specs=vmem,
        out_shape=jax.ShapeDtypeStruct((occ_i, orbitals // 2, wide), jnp.float32),
        scratch_shapes=[
            pltpu.VMEM((pairs, occ_i, kks, virt_a, LANES), jnp.bfloat16),
            pltpu.VMEM((kks * width, wide), jnp.bfloat16),
            pltpu.VMEM((occ_i, pairs, virt_a, wide), jnp.float32),
            pltpu.VMEM((occ_i, pairs // 2, virt_a, wide), jnp.float32),
            pltpu.VMEM((virt_a, kks * width), jnp.bfloat16),
            pltpu.VMEM((virt_c * occ_j, LANES), jnp.float32),
            pltpu.VMEM((SLABS, virt_c, occ_j, orbitals), jnp.bfloat16),
            pltpu.SemaphoreType.DMA((SLABS,)),
            pltpu.SemaphoreType.DMA((occ_i, 5)),
            pltpu.SemaphoreType.DMA((occ_i, pairs)),
            pltpu.SemaphoreType.DMA((occ_i, pairs // 2)),
            pltpu.SemaphoreType.DMA((occ_i, pairs // 2)),
        ],
        compiler_params=pltpu.CompilerParams(
            vmem_limit_bytes=VMEM_LIMIT, collective_id=pack, has_side_effects=True
        ),
        cost_estimate=pl.CostEstimate(
            flops=2 * integrals.size * 256, bytes_accessed=2 * integrals.size, transcendentals=0
        ),
        name="cycle",
    )(
        occ_irrep,
        sym_i,
        sym_a[:, None] ^ sym_c[None, :],
        sym_c[:, None, None] ^ sym_j[None, :, None] ^ virt_irrep[None, None, :],
        rows.reshape(occ_i, pairs, virt_a, 1),
        cols,
        fold_c,
        fold_b,
        unfold_c,
        amplitudes,
        integrals,
    )

    virt_v = total.shape[1]
    rows_v = lax.dynamic_slice_in_dim(rows, lax.axis_index("virt") * virt_v, virt_v, axis=1)
    cols_b = (sym_j[:, None] ^ virt_irrep[None, :])[:, None, :]
    unfold_b = one_hot(slot_b, cap, pack).transpose(0, 2, 1)
    unfold_b = jnp.concatenate([unfold_b, unfold_b], axis=1)
    return pl.pallas_call(
        functools.partial(unfold_kernel, pack),
        grid=(occ_i,),
        in_specs=[
            pl.BlockSpec((1, virt_v, 1), lambda i: (i, 0, 0)),
            whole(occ_j, 1, orbitals),
            pl.BlockSpec((1, virt_v, occ_j * cap), lambda i: (i, 0, 0)),
            whole(pack, 2 * LANES, orbitals),
        ],
        out_specs=pl.BlockSpec((virt_v, 1, occ_j, orbitals), lambda i: (0, i, 0, 0)),
        out_shape=jax.ShapeDtypeStruct((virt_v, occ_i, occ_j, orbitals), jnp.float32),
        compiler_params=params(),
        name="unfold",
    )(rows_v, cols_b, total, unfold_b)


def shards(mesh, amplitudes, integrals, occ_irrep, virt_irrep):
    occ_local, occs, virt_pair, virt_slice = amplitudes.shape
    occ_pair = integrals.shape[2]
    sym_i = lax.dynamic_slice_in_dim(occ_irrep, lax.axis_index("rep") * occ_local, occ_local)
    sym_a = lax.dynamic_slice_in_dim(virt_irrep, lax.axis_index("pair") * virt_pair, virt_pair)
    sym_c = lax.dynamic_slice_in_dim(virt_irrep, lax.axis_index("virt") * virt_slice, virt_slice)
    sym_j = lax.dynamic_slice_in_dim(occ_irrep, lax.axis_index("pair") * occ_pair, occ_pair)
    args = (amplitudes, integrals, sym_i, sym_a, sym_c, sym_j, occ_irrep, virt_irrep)
    fits = (
        mesh.shape["virt"] == 2
        and mesh.shape["pair"] == 4
        and occ_pair % 8 == 0
        and virt_pair % 32 == 0
        and virt_slice % 64 == 0
        and occs % 4 == 0
        and virt_irrep.shape[0] % LANES == 0
    )
    if not fits:
        return dense(*args)
    labels = jnp.arange(8, dtype=jnp.int32)
    largest = jnp.max(jnp.sum((virt_irrep[None, :] == labels[:, None]).astype(jnp.int32), axis=1))
    branch = (largest > 64).astype(jnp.int32) + (largest > 128).astype(jnp.int32)
    return lax.switch(
        branch, [functools.partial(folded, 64), functools.partial(folded, 128), dense], *args
    )


def solution(mesh):
    return jax.shard_map(
        functools.partial(shards, mesh),
        mesh=mesh,
        in_specs=(
            P(("mol", "rep"), None, "pair", "virt"),
            P("mol", "virt", "pair", None),
            P(),
            P(),
        ),
        out_specs=P("virt", ("mol", "rep"), "pair", None),
        check_vma=False,
    )
```
